32 devices in a mesh: band: 8 (over z, x), slab: 4 (over y, core).
Axes of the slice: x: 2, y: 2, z: 4, core: 2. Of those that a mesh axis runs over, the one named last changes fastest.
Arguments:
- orbitals: float32 [16, 128, 128, 128], P('band', 'slab'), may hold values from -6 to 6
- slot_ids: int32 [16], P('band'), may hold values from 0 to 15, each once
- occupations: float32 [16], replicated, may hold values from 0.25 to 2
- mode_lists: int32 [3, 48], replicated, may hold values from 0 to 127, as said below
Outputs:
- exchange_terms: float32 [16, 128, 128, 128], P('band', 'slab')
The draws below stay inside these ranges and needn't reach their ends.
Inputs may be any that keep to these rules, and one draw needn't show every extreme that they name: `slot_ids`: each number appears once. `mode_lists`: each row lists 48 different mode numbers, among them 0 and 127.
All inputs are finite; a program needn't handle non-finite values.
Results may differ from the reference program's by a relative error of at most 0.000059.
Values sent between devices are 32-bit elements; how exact they have to be, the bound alone decides.
A program may use at most 128 MiB of HBM per device.

```python
import math
import jax
import jax.numpy as jnp
from jax import lax

NG = 128
KM = 48
ORBITALS = 16


def draw_mode_lists(key, part):
    listing = []
    for dimension in range(3):
        row_key = jax.random.fold_in(key, 17 + dimension)
        first_key, second_key = jax.random.split(row_key)
        inner = jax.random.permutation(first_key, NG - 2)[:KM - 2].astype(jnp.int32) + 1
        listed = jnp.concatenate([jnp.array([0, NG - 1], dtype=jnp.int32), inner])
        order = jax.random.permutation(second_key, KM)
        listing.append(listed[order])
    return jnp.stack(listing).astype(jnp.int32)


def block_levels(own_key, shape, cuts, least, largest):
    factor_of, own = 1.0, jax.random.fold_in(own_key, 6)
    for dim, parts in cuts:
        steps = jnp.exp(jax.random.uniform(jax.random.fold_in(own, dim), (parts,), jnp.float32, least / len(cuts), largest / len(cuts)))
        factor_of = factor_of * jnp.repeat(steps, shape[dim] // parts).reshape([-1 if axis == dim else 1 for axis in range(len(shape))])
    return factor_of


def centred(stream_key, dims, spread, bound, pieces=(), held_as=jnp.bfloat16):
    entries = spread * jax.random.normal(stream_key, dims, jnp.float32)
    if pieces:
        entries = entries * block_levels(stream_key, dims, pieces, -0.22, 0.18)
    return jnp.clip(entries, -bound, bound).astype(held_as)


def setup_inputs(seed: int = 0) -> dict:
    arg_keys = jax.random.split(jax.random.key(seed), 5)
    return {
        "orbitals": centred(arg_keys[0], (ORBITALS, NG, NG, NG), 1.0, 6.0, ((0, 8), (1, 4)), jnp.float32),
        "slot_ids": jax.random.permutation(arg_keys[1], ORBITALS).astype(jnp.int32),
        "occupations": jnp.clip(jnp.exp(jax.random.uniform(arg_keys[2], (ORBITALS,), jnp.float32, math.log(0.25), math.log(2.0))), 0.25, 2.0),
        "mode_lists": draw_mode_lists(jax.random.fold_in(arg_keys[4], 71), 0),
    }


def sine_table(mode_row, points):
    grid = jnp.arange(points, dtype=jnp.int32) + 1
    phase = grid[:, None] * (mode_row[None, :].astype(jnp.int32) + 1) % (2 * points + 2)
    angle = jnp.pi * phase.astype(jnp.float32) / (points + 1.0)
    return jnp.sqrt(jnp.float32(2.0) / (points + 1.0)) * jnp.sin(angle)

def screen_table(first, second, third, points):
    squares = ((first + 1) ** 2)[:, None, None] + ((second + 1) ** 2)[None, :, None] + ((third + 1) ** 2)[None, None, :]
    return 1.0 / (1.0 + squares.astype(jnp.float32) / jnp.float32(points * points))

def reference(orbitals, slot_ids, occupations, mode_lists):
    highest = lax.Precision.HIGHEST
    slot_weight = occupations[slot_ids]
    sine_first = sine_table(mode_lists[0], NG)
    sine_second = sine_table(mode_lists[1], NG)
    sine_third = sine_table(mode_lists[2], NG)
    screen = screen_table(mode_lists[0], mode_lists[1], mode_lists[2], NG)

    def one_slot(index):
        density = orbitals[index][None] * orbitals
        coeff = jnp.einsum('jxyz,zc->jxyc', density, sine_third, precision=highest)
        coeff = jnp.einsum('jxyc,yb->jxbc', coeff, sine_second, precision=highest)
        coeff = jnp.einsum('jxbc,xa->jabc', coeff, sine_first, precision=highest)
        coeff = coeff * screen[None]
        field = jnp.einsum('jabc,xa->jxbc', coeff, sine_first, precision=highest)
        field = jnp.einsum('jxbc,yb->jxyc', field, sine_second, precision=highest)
        field = jnp.einsum('jxyc,zc->jxyz', field, sine_third, precision=highest)
        return lax.optimization_barrier(jnp.sum(slot_weight[:, None, None, None] * orbitals * field, axis=0))
    return lax.map(one_slot, jnp.arange(orbitals.shape[0], dtype=jnp.int32))
```

```python
import functools
import math

import jax
import jax.numpy as jnp
import numpy as np
from jax import lax
from jax.experimental import pallas as pl
from jax.experimental.pallas import tpu as pltpu
from jax.sharding import PartitionSpec as P

LANES = 128
ROWS = 8


def passed_along(value, axis, steps):
    count = lax.axis_size(axis)
    pairs = [(source, (source + steps) % count) for source in range(count)]
    return lax.ppermute(value, axis, pairs)


def sine_table(mode_row, points):
    grid = jnp.arange(points, dtype=jnp.int32) + 1
    phase = grid[:, None] * (mode_row[None, :] + 1) % (2 * points + 2)
    angle = jnp.pi * phase.astype(jnp.float32) / (points + 1.0)
    return jnp.sqrt(jnp.float32(2.0) / (points + 1.0)) * jnp.sin(angle)


def screen_table(first, second, third, points):
    squares = (
        ((first + 1) ** 2)[:, None, None]
        + ((second + 1) ** 2)[None, :, None]
        + ((third + 1) ** 2)[None, None, :]
    )
    return 1.0 / (1.0 + squares.astype(jnp.float32) / jnp.float32(points * points))


def visiting_form(orbitals, slot_ids, occupations, mode_lists):
    highest = lax.Precision.HIGHEST
    planes = orbitals.shape[1]
    points = orbitals.shape[2]
    count = mode_lists.shape[1]
    groups = lax.axis_size("slab")
    share = count // groups
    width = share * count
    sine_first = sine_table(mode_lists[0], points)
    sine_second = sine_table(mode_lists[1], points)
    sine_third = sine_table(mode_lists[2], points)
    local_modes = lax.dynamic_slice_in_dim(mode_lists[1], lax.axis_index("slab") * share, share)
    screen_local = screen_table(mode_lists[0], local_modes, mode_lists[2], points).reshape(
        count, width
    )
    catalog = jnp.arange(occupations.shape[0], dtype=jnp.int32)
    own_weight = jnp.sum(
        jnp.where(slot_ids[:, None] == catalog[None, :], occupations[None, :], 0.0), axis=1
    )
    own_scaled = own_weight[:, None, None, None] * orbitals

    def modal(block):
        items = block.shape[0]
        flat = block.reshape(items, points, width)
        spectral = (
            jnp.einsum("nxc,xa->nac", flat, sine_first, precision=highest) * screen_local[None]
        )
        spatial = jnp.einsum("nac,xa->nxc", spectral, sine_first, precision=highest)
        spatial = spatial.reshape(items, points, 1, width)
        return lax.all_to_all(spatial, "slab", split_axis=1, concat_axis=2, tiled=True)

    def pair_solve(left, right):
        lead = left.shape[0]
        other = right.shape[0]
        pairs = lead * other
        density = (left[:, None] * right[None, :]).reshape(pairs * planes * points, points)
        coeffs = jnp.dot(density, sine_third, precision=highest).reshape(
            pairs, planes, points, count
        )
        coeffs = jnp.einsum("nxyk,yj->nxjk", coeffs, sine_second, precision=highest)
        coeffs = coeffs.reshape(pairs, planes, groups, width)
        returned = modal(lax.all_to_all(coeffs, "slab", split_axis=2, concat_axis=1, tiled=True))
        returned = returned.reshape(pairs, planes, count, count)
        field = jnp.einsum("nxjk,yj->nxyk", returned, sine_second, precision=highest)
        field = jnp.dot(
            field.reshape(pairs * planes * points, count), sine_third.T, precision=highest
        )
        return field.reshape(lead, other, planes, points, points)

    def gathered(field, visitors, visit_weight):
        return jnp.sum(field * (visit_weight[:, None, None, None] * visitors)[None], axis=1)

    field = pair_solve(orbitals, orbitals)
    totals = jnp.sum(field * own_scaled[None], axis=1)
    bands = lax.axis_size("band")
    half = bands // 2
    visitors, visit_weight = passed_along((orbitals, own_weight), "band", 1)
    field = pair_solve(orbitals, visitors)
    totals = totals + gathered(field, visitors, visit_weight)
    carried = jnp.sum(field * own_scaled[:, None], axis=0)

    def carry_step(step_index, carry):
        running, visitors, visit_weight, partial_terms = carry
        visitors, visit_weight, partial_terms = passed_along(
            (visitors, visit_weight, partial_terms), "band", 1
        )
        solved = pair_solve(orbitals, visitors)
        running = running + gathered(solved, visitors, visit_weight)
        partial_terms = partial_terms + jnp.sum(solved * own_scaled[:, None], axis=0)
        return (running, visitors, visit_weight, partial_terms)

    totals, visitors, visit_weight, carried = lax.fori_loop(
        2, half, carry_step, (totals, visitors, visit_weight, carried)
    )
    home_terms = passed_along(carried, "band", 1 - half)
    visitors, visit_weight = passed_along((visitors, visit_weight), "band", 1)
    field = pair_solve(orbitals, visitors)
    totals = totals + gathered(field, visitors, visit_weight) + home_terms
    return totals


def split_two(value):
    high = value.astype(jnp.bfloat16)
    return high, (value - high.astype(jnp.float32)).astype(jnp.bfloat16)


def split_table(value):
    high = lax.reduce_precision(value, exponent_bits=8, mantissa_bits=7)
    return high.astype(jnp.bfloat16), (value - high).astype(jnp.bfloat16)


def mxu(left, right):
    return jnp.dot(left, right, preferred_element_type=jnp.float32)


def windows(count):
    pack = LANES // math.gcd(count, LANES)
    tiles = pack * count // LANES
    return [min(2 * k * count // LANES, tiles - 2) for k in range(pack // 2)], pack, tiles


def forward_kernel(firsts, seconds, orbs, left, place_high, place_low, out):
    planes = orbs.shape[1]
    count = left.shape[0] // 2
    starts, pack, lane_tiles = windows(count)
    row_tiles = count // ROWS
    per_group = lane_tiles * row_tiles
    share = out.shape[2]
    groups = firsts.shape[0] // pack

    for tile in range(groups * per_group, out.shape[0] * share):
        out[tile // share, :, tile % share] = jnp.zeros((planes,) + out.shape[3:], jnp.float32)

    def group_step(group, _):
        sums = [None] * lane_tiles
        for couple, start in enumerate(starts):
            rows = []
            for plane in range(planes):
                sides = []
                for member in range(2):
                    slot = group * pack + 2 * couple + member
                    sides.append(orbs[firsts[slot], plane] * orbs[seconds[slot], plane])
                high, low = split_two(jnp.concatenate(sides, axis=1))
                half = mxu(left[...], jnp.concatenate([high, low], axis=0))
                rows.append(half[:count] + half[count:])
            high, low = split_two(jnp.concatenate(rows, axis=0))
            done = (
                mxu(high, place_high[couple])
                + mxu(low, place_high[couple])
                + mxu(high, place_low[couple])
            )
            for side in range(2):
                part = done[:, side * LANES : (side + 1) * LANES]
                held = sums[start + side]
                sums[start + side] = part if held is None else held + part
        for lane_tile in range(lane_tiles):
            for row_tile in range(row_tiles):
                tile = group * per_group + lane_tile * row_tiles + row_tile
                for plane in range(planes):
                    row = plane * count + row_tile * ROWS
                    out[tile // share, plane, tile % share] = sums[lane_tile][row : row + ROWS]
        return 0

    lax.fori_loop(0, groups, group_step, 0)


def inverse_kernel(firsts, seconds, weights, field, orbs, left, place_high, place_low, out):
    planes = orbs.shape[1]
    count = left.shape[1] // 3
    starts, pack, lane_tiles = windows(count)
    row_tiles = count // ROWS
    per_group = lane_tiles * row_tiles
    share = field.shape[2]
    groups = firsts.shape[0] // pack
    points = orbs.shape[3]

    out[...] = jnp.zeros(out.shape, out.dtype)

    def group_step(group, _):
        parts = []
        for lane_tile in range(lane_tiles):
            rows = []
            for plane in range(planes):
                for row_tile in range(row_tiles):
                    tile = group * per_group + lane_tile * row_tiles + row_tile
                    rows.append(field[tile // share, plane, tile % share])
            parts.append(split_two(jnp.concatenate(rows, axis=0)))
        for couple, start in enumerate(starts):
            high = jnp.concatenate([parts[start][0], parts[start + 1][0]], axis=1)
            low = jnp.concatenate([parts[start][1], parts[start + 1][1]], axis=1)
            half_high, half_low = split_two(
                mxu(high, place_high[couple])
                + mxu(low, place_high[couple])
                + mxu(high, place_low[couple])
            )
            for plane in range(planes):
                span = slice(plane * count, (plane + 1) * count)
                stacked = jnp.concatenate(
                    [half_high[span], half_low[span], half_high[span]], axis=0
                )
                solved = mxu(left[...], stacked)
                for member in range(2):
                    slot = group * pack + 2 * couple + member
                    one, two = firsts[slot], seconds[slot]
                    potential = solved[:, member * points : (member + 1) * points]
                    twice = jnp.where(one == two, 0.0, weights[one])
                    out[one, plane] += potential * orbs[two, plane] * weights[two]
                    out[two, plane] += potential * orbs[one, plane] * twice
        return 0

    lax.fori_loop(0, groups, group_step, 0)


def spread_form(orbitals, slot_ids, occupations, mode_lists):
    bands, slabs = lax.axis_size("band"), lax.axis_size("slab")
    devices = bands * slabs
    points = orbitals.shape[2]
    total = orbitals.shape[0] * bands
    planes = orbitals.shape[1] // bands
    count = mode_lists.shape[1]
    sine_first = sine_table(mode_lists[0], points)
    sine_second = sine_table(mode_lists[1], points)
    sine_third = sine_table(mode_lists[2], points)
    starts, pack, lane_tiles = windows(count)
    row_tiles = count // ROWS
    per_group = lane_tiles * row_tiles

    pairs = [(i, j) for i in range(total) for j in range(i, total)]
    groups = len(pairs) // pack
    share = -(-groups * per_group // devices)
    firsts = jnp.asarray(np.array([p[0] for p in pairs], np.int32))
    seconds = jnp.asarray(np.array([p[1] for p in pairs], np.int32))

    catalog = jnp.arange(occupations.shape[0], dtype=jnp.int32)
    own_weight = jnp.sum(
        jnp.where(slot_ids[:, None] == catalog[None, :], occupations[None, :], 0.0), axis=1
    )
    weights = lax.all_gather(own_weight, "band", tiled=True)

    spread = lax.all_to_all(orbitals, "band", split_axis=1, concat_axis=0, tiled=True)

    second_high, second_low = split_table(sine_second)
    empty = jnp.zeros_like(second_low)
    forward_left = jnp.concatenate(
        [
            jnp.concatenate([second_high, second_high], axis=0),
            jnp.concatenate([second_low, empty], axis=0),
        ],
        axis=1,
    ).T
    inverse_left = jnp.concatenate([second_high, second_high, second_low], axis=1)
    placed = []
    block = jnp.kron(jnp.eye(2, dtype=jnp.float32), sine_third.T)
    for couple, start in enumerate(starts):
        above = 2 * couple * count - start * LANES
        placed.append(jnp.pad(block, ((above, 2 * LANES - above - 2 * count), (0, 0))))
    inverse_place = split_table(jnp.stack(placed))
    forward_place = [part.swapaxes(1, 2) for part in inverse_place]

    vmem = pl.BlockSpec(memory_space=pltpu.VMEM)
    smem = pl.BlockSpec(memory_space=pltpu.SMEM)
    params = pltpu.CompilerParams(vmem_limit_bytes=50 * 2**20)
    modal_shape = (devices, planes, share, ROWS, LANES)
    coeffs = pl.pallas_call(
        forward_kernel,
        out_shape=jax.ShapeDtypeStruct(modal_shape, jnp.float32),
        in_specs=[smem, smem] + [vmem] * 4,
        out_specs=vmem,
        compiler_params=params,
    )(firsts, seconds, spread, forward_left, *forward_place)

    both = ("band", "slab")
    coeffs = lax.all_to_all(coeffs, both, split_axis=0, concat_axis=0, tiled=True)

    first_sent = (
        sine_first.reshape(slabs, bands, planes, count).swapaxes(0, 1).reshape(points, count)
    )
    squares = [(mode_lists[d] + 1) ** 2 for d in range(3)]
    inner = (
        squares[1].reshape(1, row_tiles, ROWS, 1)
        + jnp.tile(squares[2], pack).reshape(lane_tiles, 1, 1, LANES)
    ).reshape(per_group, ROWS, LANES)
    rounds = -(-share // per_group) + 1
    device = lax.axis_index("band") * slabs + lax.axis_index("slab")
    inner = lax.dynamic_slice_in_dim(
        jnp.tile(inner, (rounds, 1, 1)), lax.rem(device * share, per_group), share
    )
    both_squares = (squares[0][:, None] + inner.reshape(1, -1)).astype(jnp.float32)
    screen = 1.0 / (1.0 + both_squares / jnp.float32(points * points))
    flat = coeffs.reshape(points, share * ROWS * LANES)
    spectral = screen * jnp.einsum("xm,xa->am", flat, first_sent, precision=lax.Precision.HIGH)
    spatial = jnp.einsum("am,xa->xm", spectral, first_sent, precision=lax.Precision.HIGH)
    spatial = spatial.reshape(modal_shape)
    field = lax.all_to_all(spatial, both, split_axis=0, concat_axis=0, tiled=True)

    terms = pl.pallas_call(
        inverse_kernel,
        out_shape=jax.ShapeDtypeStruct(spread.shape, jnp.float32),
        in_specs=[smem] * 3 + [vmem] * 5,
        out_specs=vmem,
        compiler_params=params,
    )(firsts, seconds, weights, field, spread, inverse_left, *inverse_place)
    return lax.all_to_all(terms, "band", split_axis=0, concat_axis=1, tiled=True)


def on_device(orbitals, slot_ids, occupations, mode_lists):
    total = orbitals.shape[0] * lax.axis_size("band")
    points, count = orbitals.shape[2], mode_lists.shape[1]
    pack = LANES // math.gcd(count, LANES)
    fits = (
        orbitals.shape[1] % lax.axis_size("band") == 0
        and points == LANES
        and count % 16 == 0
        and pack * count >= 2 * LANES
        and (total * (total + 1) // 2) % pack == 0
    )
    form = spread_form if fits else visiting_form
    return form(orbitals, slot_ids, occupations, mode_lists)


def solution(mesh):
    in_specs = (P("band", "slab", None, None), P("band"), P(), P())
    out_specs = P("band", "slab", None, None)
    return jax.shard_map(
        on_device, mesh=mesh, in_specs=in_specs, out_specs=out_specs, check_vma=False
    )
```

```python
import functools
import math

import jax
import jax.numpy as jnp
import numpy as np
from jax import lax
from jax.experimental import pallas as pl
from jax.experimental.pallas import tpu as pltpu
from jax.sharding import PartitionSpec as P

LANES = 128
ROWS = 8


def passed_along(value, axis, steps):
    count = lax.axis_size(axis)
    pairs = [(source, (source + steps) % count) for source in range(count)]
    return lax.ppermute(value, axis, pairs)


def sine_table(mode_row, points):
    grid = jnp.arange(points, dtype=jnp.int32) + 1
    phase = grid[:, None] * (mode_row[None, :] + 1) % (2 * points + 2)
    angle = jnp.pi * phase.astype(jnp.float32) / (points + 1.0)
    return jnp.sqrt(jnp.float32(2.0) / (points + 1.0)) * jnp.sin(angle)


def screen_table(first, second, third, points):
    squares = (
        ((first + 1) ** 2)[:, None, None]
        + ((second + 1) ** 2)[None, :, None]
        + ((third + 1) ** 2)[None, None, :]
    )
    return 1.0 / (1.0 + squares.astype(jnp.float32) / jnp.float32(points * points))


def visiting_form(orbitals, slot_ids, occupations, mode_lists):
    highest = lax.Precision.HIGHEST
    planes = orbitals.shape[1]
    points = orbitals.shape[2]
    count = mode_lists.shape[1]
    groups = lax.axis_size("slab")
    share = count // groups
    width = share * count
    sine_first = sine_table(mode_lists[0], points)
    sine_second = sine_table(mode_lists[1], points)
    sine_third = sine_table(mode_lists[2], points)
    local_modes = lax.dynamic_slice_in_dim(mode_lists[1], lax.axis_index("slab") * share, share)
    screen_local = screen_table(mode_lists[0], local_modes, mode_lists[2], points).reshape(
        count, width
    )
    catalog = jnp.arange(occupations.shape[0], dtype=jnp.int32)
    own_weight = jnp.sum(
        jnp.where(slot_ids[:, None] == catalog[None, :], occupations[None, :], 0.0), axis=1
    )
    own_scaled = own_weight[:, None, None, None] * orbitals

    def modal(block):
        items = block.shape[0]
        flat = block.reshape(items, points, width)
        spectral = (
            jnp.einsum("nxc,xa->nac", flat, sine_first, precision=highest) * screen_local[None]
        )
        spatial = jnp.einsum("nac,xa->nxc", spectral, sine_first, precision=highest)
        spatial = spatial.reshape(items, points, 1, width)
        return lax.all_to_all(spatial, "slab", split_axis=1, concat_axis=2, tiled=True)

    def pair_solve(left, right):
        lead = left.shape[0]
        other = right.shape[0]
        pairs = lead * other
        density = (left[:, None] * right[None, :]).reshape(pairs * planes * points, points)
        coeffs = jnp.dot(density, sine_third, precision=highest).reshape(
            pairs, planes, points, count
        )
        coeffs = jnp.einsum("nxyk,yj->nxjk", coeffs, sine_second, precision=highest)
        coeffs = coeffs.reshape(pairs, planes, groups, width)
        returned = modal(lax.all_to_all(coeffs, "slab", split_axis=2, concat_axis=1, tiled=True))
        returned = returned.reshape(pairs, planes, count, count)
        field = jnp.einsum("nxjk,yj->nxyk", returned, sine_second, precision=highest)
        field = jnp.dot(
            field.reshape(pairs * planes * points, count), sine_third.T, precision=highest
        )
        return field.reshape(lead, other, planes, points, points)

    def gathered(field, visitors, visit_weight):
        return jnp.sum(field * (visit_weight[:, None, None, None] * visitors)[None], axis=1)

    field = pair_solve(orbitals, orbitals)
    totals = jnp.sum(field * own_scaled[None], axis=1)
    bands = lax.axis_size("band")
    half = bands // 2
    visitors, visit_weight = passed_along((orbitals, own_weight), "band", 1)
    field = pair_solve(orbitals, visitors)
    totals = totals + gathered(field, visitors, visit_weight)
    carried = jnp.sum(field * own_scaled[:, None], axis=0)

    def carry_step(step_index, carry):
        running, visitors, visit_weight, partial_terms = carry
        visitors, visit_weight, partial_terms = passed_along(
            (visitors, visit_weight, partial_terms), "band", 1
        )
        solved = pair_solve(orbitals, visitors)
        running = running + gathered(solved, visitors, visit_weight)
        partial_terms = partial_terms + jnp.sum(solved * own_scaled[:, None], axis=0)
        return (running, visitors, visit_weight, partial_terms)

    totals, visitors, visit_weight, carried = lax.fori_loop(
        2, half, carry_step, (totals, visitors, visit_weight, carried)
    )
    home_terms = passed_along(carried, "band", 1 - half)
    visitors, visit_weight = passed_along((visitors, visit_weight), "band", 1)
    field = pair_solve(orbitals, visitors)
    totals = totals + gathered(field, visitors, visit_weight) + home_terms
    return totals


def split_two(value):
    high = value.astype(jnp.bfloat16)
    return high, (value - high.astype(jnp.float32)).astype(jnp.bfloat16)


def split_table(value):
    high = lax.reduce_precision(value, exponent_bits=8, mantissa_bits=7)
    return high.astype(jnp.bfloat16), (value - high).astype(jnp.bfloat16)


def mxu(left, right):
    return jnp.dot(left, right, preferred_element_type=jnp.float32)


def windows(count):
    pack = LANES // math.gcd(count, LANES)
    tiles = pack * count // LANES
    return [min(2 * k * count // LANES, tiles - 2) for k in range(pack // 2)], pack, tiles


def forward_kernel(firsts, seconds, orbs, others, left, place_high, place_low, out):
    planes = orbs.shape[1]
    count = left.shape[0] // 2
    starts, pack, lane_tiles = windows(count)
    row_tiles = count // ROWS
    per_group = lane_tiles * row_tiles
    share = out.shape[2]
    groups = firsts.shape[0] // pack

    for tile in range(groups * per_group, out.shape[0] * share):
        out[tile // share, :, tile % share] = jnp.zeros((planes,) + out.shape[3:], jnp.float32)

    def group_step(group, _):
        sums = [None] * lane_tiles
        for couple, start in enumerate(starts):
            rows = []
            for plane in range(planes):
                sides = []
                for member in range(2):
                    slot = group * pack + 2 * couple + member
                    sides.append(orbs[firsts[slot], plane] * others[seconds[slot], plane])
                high, low = split_two(jnp.concatenate(sides, axis=1))
                half = mxu(left[...], jnp.concatenate([high, low], axis=0))
                rows.append(half[:count] + half[count:])
            high, low = split_two(jnp.concatenate(rows, axis=0))
            done = (
                mxu(high, place_high[couple])
                + mxu(low, place_high[couple])
                + mxu(high, place_low[couple])
            )
            for side in range(2):
                part = done[:, side * LANES : (side + 1) * LANES]
                held = sums[start + side]
                sums[start + side] = part if held is None else held + part
        for lane_tile in range(lane_tiles):
            for row_tile in range(row_tiles):
                tile = group * per_group + lane_tile * row_tiles + row_tile
                for plane in range(planes):
                    row = plane * count + row_tile * ROWS
                    out[tile // share, plane, tile % share] = sums[lane_tile][row : row + ROWS]
        return 0

    lax.fori_loop(0, groups, group_step, 0)


def inverse_kernel(mutual, firsts, seconds, scale_one, scale_two, field, orbs, others, *rest):
    *base, left, place_high, place_low, out = rest
    planes = orbs.shape[1]
    count = left.shape[1] // 3
    starts, pack, lane_tiles = windows(count)
    row_tiles = count // ROWS
    per_group = lane_tiles * row_tiles
    share = field.shape[2]
    groups = firsts.shape[0] // pack
    points = orbs.shape[3]

    out[...] = base[0][...] if base else jnp.zeros(out.shape, out.dtype)

    def group_step(group, _):
        parts = []
        for lane_tile in range(lane_tiles):
            rows = []
            for plane in range(planes):
                for row_tile in range(row_tiles):
                    tile = group * per_group + lane_tile * row_tiles + row_tile
                    rows.append(field[tile // share, plane, tile % share])
            parts.append(split_two(jnp.concatenate(rows, axis=0)))
        for couple, start in enumerate(starts):
            high = jnp.concatenate([parts[start][0], parts[start + 1][0]], axis=1)
            low = jnp.concatenate([parts[start][1], parts[start + 1][1]], axis=1)
            half_high, half_low = split_two(
                mxu(high, place_high[couple])
                + mxu(low, place_high[couple])
                + mxu(high, place_low[couple])
            )
            for plane in range(planes):
                span = slice(plane * count, (plane + 1) * count)
                stacked = jnp.concatenate(
                    [half_high[span], half_low[span], half_high[span]], axis=0
                )
                solved = mxu(left[...], stacked)
                for member in range(2):
                    slot = group * pack + 2 * couple + member
                    one, two = firsts[slot], seconds[slot]
                    potential = solved[:, member * points : (member + 1) * points]
                    out[one, plane] += potential * others[two, plane] * scale_one[slot]
                    if mutual:
                        out[two, plane] += potential * orbs[one, plane] * scale_two[slot]
        return 0

    lax.fori_loop(0, groups, group_step, 0)


def spread_form(orbitals, slot_ids, occupations, mode_lists):
    bands, slabs = lax.axis_size("band"), lax.axis_size("slab")
    half = bands // 2
    devices = half * slabs
    points = orbitals.shape[2]
    local = orbitals.shape[0]
    own = local * half
    planes = orbitals.shape[1] // half
    count = mode_lists.shape[1]
    sine_first = sine_table(mode_lists[0], points)
    sine_second = sine_table(mode_lists[1], points)
    sine_third = sine_table(mode_lists[2], points)
    starts, pack, lane_tiles = windows(count)
    row_tiles = count // ROWS
    per_group = lane_tiles * row_tiles
    band, slab = lax.axis_index("band"), lax.axis_index("slab")
    sides = [[side * half + member for member in range(half)] for side in range(2)]
    all_sides = [
        [member * slabs + other for member in side for other in range(slabs)] for side in sides
    ]
    both = ("band", "slab")

    def to_planes(value):
        return lax.all_to_all(
            value, "band", split_axis=1, concat_axis=0, tiled=True, axis_index_groups=sides
        )

    def exchanged(value):
        return lax.all_to_all(
            value, both, split_axis=0, concat_axis=0, tiled=True, axis_index_groups=all_sides
        )

    visiting = [passed_along(orbitals[k : k + 1], "band", half) for k in range(local)]
    mine = to_planes(orbitals)
    visiting = [to_planes(value) for value in visiting]

    catalog = jnp.arange(occupations.shape[0], dtype=jnp.int32)
    own_weight = jnp.sum(
        jnp.where(slot_ids[:, None] == catalog[None, :], occupations[None, :], 0.0), axis=1
    )
    weights = lax.all_gather(own_weight, "band", tiled=True).reshape(2, own)
    upper = band >= half
    my_weights = jnp.where(upper, weights[1], weights[0])
    other_weights = jnp.where(upper, weights[0], weights[1]).reshape(half, local)

    second_high, second_low = split_table(sine_second)
    empty = jnp.zeros_like(second_low)
    forward_left = jnp.concatenate(
        [
            jnp.concatenate([second_high, second_high], axis=0),
            jnp.concatenate([second_low, empty], axis=0),
        ],
        axis=1,
    ).T
    inverse_left = jnp.concatenate([second_high, second_high, second_low], axis=1)
    placed = []
    block = jnp.kron(jnp.eye(2, dtype=jnp.float32), sine_third.T)
    for couple, start in enumerate(starts):
        above = 2 * couple * count - start * LANES
        placed.append(jnp.pad(block, ((above, 2 * LANES - above - 2 * count), (0, 0))))
    inverse_place = split_table(jnp.stack(placed))
    forward_place = [part.swapaxes(1, 2) for part in inverse_place]

    first_sent = (
        sine_first.reshape(slabs, half, planes, count).swapaxes(0, 1).reshape(points, count)
    )
    squares = [(mode_lists[d] + 1) ** 2 for d in range(3)]
    inner_tiles = (
        squares[1].reshape(1, row_tiles, ROWS, 1)
        + jnp.tile(squares[2], pack).reshape(lane_tiles, 1, 1, LANES)
    ).reshape(per_group, ROWS, LANES)
    device = lax.rem(band, half) * slabs + slab

    vmem = pl.BlockSpec(memory_space=pltpu.VMEM)
    smem = pl.BlockSpec(memory_space=pltpu.SMEM)
    params = pltpu.CompilerParams(vmem_limit_bytes=50 * 2**20)

    def modal(coeffs):
        share = coeffs.shape[2]
        rounds = -(-share // per_group) + 1
        inner = lax.dynamic_slice_in_dim(
            jnp.tile(inner_tiles, (rounds, 1, 1)), lax.rem(device * share, per_group), share
        )
        both_squares = (squares[0][:, None] + inner.reshape(1, -1)).astype(jnp.float32)
        screen = 1.0 / (1.0 + both_squares / jnp.float32(points * points))
        flat = exchanged(coeffs).reshape(points, share * ROWS * LANES)
        spectral = screen * jnp.einsum(
            "xm,xa->am", flat, first_sent, precision=lax.Precision.HIGH
        )
        spatial = jnp.einsum("am,xa->xm", spectral, first_sent, precision=lax.Precision.HIGH)
        return exchanged(spatial.reshape(coeffs.shape))

    def pair_cost(pairs):
        work = pairs * planes * points * points * 2 * LANES * 4
        return pl.CostEstimate(flops=work, bytes_accessed=2**24, transcendentals=0)

    def fields_of(pairs, others):
        tables = [jnp.asarray(np.array(part, np.int32)) for part in zip(*pairs)]
        groups = len(pairs) // pack
        share = -(-groups * per_group // devices)
        coeffs = pl.pallas_call(
            forward_kernel,
            out_shape=jax.ShapeDtypeStruct((devices, planes, share, ROWS, LANES), jnp.float32),
            in_specs=[smem] * 2 + [vmem] * 5,
            out_specs=vmem,
            compiler_params=params,
            cost_estimate=pair_cost(len(pairs)),
        )(*tables, mine, others, forward_left, *forward_place)
        return tables, modal(coeffs)

    def terms_of(tables, field, others, scales, base):
        extra = [] if base is None else [base]
        return pl.pallas_call(
            functools.partial(inverse_kernel, base is None),
            out_shape=jax.ShapeDtypeStruct(mine.shape, jnp.float32),
            in_specs=[smem] * 4 + [vmem] * (6 + len(extra)),
            out_specs=vmem,
            compiler_params=params,
            cost_estimate=pair_cost(tables[0].shape[0]),
        )(*tables, *scales, field, mine, others, *extra, inverse_left, *inverse_place)

    pairs = [(i, j) for i in range(own) for j in range(i, own)]
    true_pairs = len(pairs)
    pairs += [(0, 0)] * (-true_pairs % pack)
    valid = np.arange(len(pairs)) < true_pairs
    apart = np.array([i != j for i, j in pairs])
    tables, field = fields_of(pairs, mine)
    scales = (
        jnp.where(valid, my_weights[tables[1]], 0.0),
        jnp.where(valid & apart, my_weights[tables[0]], 0.0),
    )
    cross = [(i, j) for i in range(own) for j in range(half)]
    solved = [fields_of(cross, value) for value in visiting]
    terms = terms_of(tables, field, mine, scales, None)
    for k, (tables, field) in enumerate(solved):
        scale = other_weights[:, k][tables[1]]
        terms = terms_of(tables, field, visiting[k], (scale, scale), terms)
    return lax.all_to_all(
        terms, "band", split_axis=0, concat_axis=1, tiled=True, axis_index_groups=sides
    )


def on_device(orbitals, slot_ids, occupations, mode_lists):
    bands = lax.axis_size("band")
    points, count = orbitals.shape[2], mode_lists.shape[1]
    pack = LANES // math.gcd(count, LANES)
    half = bands // 2
    fits = (
        bands % 2 == 0
        and orbitals.shape[1] % half == 0
        and points == LANES
        and count % 16 == 0
        and pack * count >= 2 * LANES
        and (orbitals.shape[0] * half * half) % pack == 0
    )
    form = spread_form if fits else visiting_form
    return form(orbitals, slot_ids, occupations, mode_lists)


def solution(mesh):
    in_specs = (P("band", "slab", None, None), P("band"), P(), P())
    out_specs = P("band", "slab", None, None)
    return jax.shard_map(
        on_device, mesh=mesh, in_specs=in_specs, out_specs=out_specs, check_vma=False
    )
```

```python
import functools
import math

import jax
import jax.numpy as jnp
import numpy as np
from jax import lax
from jax.experimental import pallas as pl
from jax.experimental.pallas import tpu as pltpu
from jax.sharding import PartitionSpec as P

LANES = 128
ROWS = 8


def passed_along(value, axis, steps):
    count = lax.axis_size(axis)
    pairs = [(source, (source + steps) % count) for source in range(count)]
    return lax.ppermute(value, axis, pairs)


def sine_table(mode_row, points):
    grid = jnp.arange(points, dtype=jnp.int32) + 1
    phase = grid[:, None] * (mode_row[None, :] + 1) % (2 * points + 2)
    angle = jnp.pi * phase.astype(jnp.float32) / (points + 1.0)
    return jnp.sqrt(jnp.float32(2.0) / (points + 1.0)) * jnp.sin(angle)


def screen_table(first, second, third, points):
    squares = (
        ((first + 1) ** 2)[:, None, None]
        + ((second + 1) ** 2)[None, :, None]
        + ((third + 1) ** 2)[None, None, :]
    )
    return 1.0 / (1.0 + squares.astype(jnp.float32) / jnp.float32(points * points))


def visiting_form(orbitals, slot_ids, occupations, mode_lists):
    highest = lax.Precision.HIGHEST
    planes = orbitals.shape[1]
    points = orbitals.shape[2]
    count = mode_lists.shape[1]
    groups = lax.axis_size("slab")
    share = count // groups
    width = share * count
    sine_first = sine_table(mode_lists[0], points)
    sine_second = sine_table(mode_lists[1], points)
    sine_third = sine_table(mode_lists[2], points)
    local_modes = lax.dynamic_slice_in_dim(mode_lists[1], lax.axis_index("slab") * share, share)
    screen_local = screen_table(mode_lists[0], local_modes, mode_lists[2], points).reshape(
        count, width
    )
    catalog = jnp.arange(occupations.shape[0], dtype=jnp.int32)
    own_weight = jnp.sum(
        jnp.where(slot_ids[:, None] == catalog[None, :], occupations[None, :], 0.0), axis=1
    )
    own_scaled = own_weight[:, None, None, None] * orbitals

    def modal(block):
        items = block.shape[0]
        flat = block.reshape(items, points, width)
        spectral = (
            jnp.einsum("nxc,xa->nac", flat, sine_first, precision=highest) * screen_local[None]
        )
        spatial = jnp.einsum("nac,xa->nxc", spectral, sine_first, precision=highest)
        spatial = spatial.reshape(items, points, 1, width)
        return lax.all_to_all(spatial, "slab", split_axis=1, concat_axis=2, tiled=True)

    def pair_solve(left, right):
        lead = left.shape[0]
        other = right.shape[0]
        pairs = lead * other
        density = (left[:, None] * right[None, :]).reshape(pairs * planes * points, points)
        coeffs = jnp.dot(density, sine_third, precision=highest).reshape(
            pairs, planes, points, count
        )
        coeffs = jnp.einsum("nxyk,yj->nxjk", coeffs, sine_second, precision=highest)
        coeffs = coeffs.reshape(pairs, planes, groups, width)
        returned = modal(lax.all_to_all(coeffs, "slab", split_axis=2, concat_axis=1, tiled=True))
        returned = returned.reshape(pairs, planes, count, count)
        field = jnp.einsum("nxjk,yj->nxyk", returned, sine_second, precision=highest)
        field = jnp.dot(
            field.reshape(pairs * planes * points, count), sine_third.T, precision=highest
        )
        return field.reshape(lead, other, planes, points, points)

    def gathered(field, visitors, visit_weight):
        return jnp.sum(field * (visit_weight[:, None, None, None] * visitors)[None], axis=1)

    field = pair_solve(orbitals, orbitals)
    totals = jnp.sum(field * own_scaled[None], axis=1)
    bands = lax.axis_size("band")
    half = bands // 2
    visitors, visit_weight = passed_along((orbitals, own_weight), "band", 1)
    field = pair_solve(orbitals, visitors)
    totals = totals + gathered(field, visitors, visit_weight)
    carried = jnp.sum(field * own_scaled[:, None], axis=0)

    def carry_step(step_index, carry):
        running, visitors, visit_weight, partial_terms = carry
        visitors, visit_weight, partial_terms = passed_along(
            (visitors, visit_weight, partial_terms), "band", 1
        )
        solved = pair_solve(orbitals, visitors)
        running = running + gathered(solved, visitors, visit_weight)
        partial_terms = partial_terms + jnp.sum(solved * own_scaled[:, None], axis=0)
        return (running, visitors, visit_weight, partial_terms)

    totals, visitors, visit_weight, carried = lax.fori_loop(
        2, half, carry_step, (totals, visitors, visit_weight, carried)
    )
    home_terms = passed_along(carried, "band", 1 - half)
    visitors, visit_weight = passed_along((visitors, visit_weight), "band", 1)
    field = pair_solve(orbitals, visitors)
    totals = totals + gathered(field, visitors, visit_weight) + home_terms
    return totals


def split_two(value):
    high = value.astype(jnp.bfloat16)
    return high, (value - high.astype(jnp.float32)).astype(jnp.bfloat16)


def split_table(value):
    high = lax.reduce_precision(value, exponent_bits=8, mantissa_bits=7)
    return high.astype(jnp.bfloat16), (value - high).astype(jnp.bfloat16)


def mxu(left, right):
    return jnp.dot(left, right, preferred_element_type=jnp.float32)


def windows(count):
    pack = LANES // math.gcd(count, LANES)
    tiles = pack * count // LANES
    return [min(2 * k * count // LANES, tiles - 2) for k in range(pack // 2)], pack, tiles


def forward_kernel(firsts, seconds, orbs, others, left, place_high, place_low, out):
    planes = orbs.shape[1]
    count = left.shape[0] // 2
    starts, pack, lane_tiles = windows(count)
    row_tiles = count // ROWS
    per_group = lane_tiles * row_tiles
    share = out.shape[2]
    groups = firsts.shape[0] // pack

    for tile in range(groups * per_group, out.shape[0] * share):
        out[tile // share, :, tile % share] = jnp.zeros((planes,) + out.shape[3:], jnp.float32)

    def group_step(group, _):
        sums = [None] * lane_tiles
        for couple, start in enumerate(starts):
            rows = []
            for plane in range(planes):
                sides = []
                for member in range(2):
                    slot = group * pack + 2 * couple + member
                    sides.append(orbs[firsts[slot], plane] * others[seconds[slot], plane])
                high, low = split_two(jnp.concatenate(sides, axis=1))
                half = mxu(left[...], jnp.concatenate([high, low], axis=0))
                rows.append(half[:count] + half[count:])
            high, low = split_two(jnp.concatenate(rows, axis=0))
            done = (
                mxu(high, place_high[couple])
                + mxu(low, place_high[couple])
                + mxu(high, place_low[couple])
            )
            for side in range(2):
                part = done[:, side * LANES : (side + 1) * LANES]
                held = sums[start + side]
                sums[start + side] = part if held is None else held + part
        for lane_tile in range(lane_tiles):
            for row_tile in range(row_tiles):
                tile = group * per_group + lane_tile * row_tiles + row_tile
                for plane in range(planes):
                    row = plane * count + row_tile * ROWS
                    out[tile // share, plane, tile % share] = sums[lane_tile][row : row + ROWS]
        return 0

    lax.fori_loop(0, groups, group_step, 0)


def inverse_kernel(true_pairs, firsts, seconds, weights, field, orbs, others, *rest):
    *base, left, place_high, place_low, out = rest
    planes = orbs.shape[1]
    count = left.shape[1] // 3
    starts, pack, lane_tiles = windows(count)
    row_tiles = count // ROWS
    per_group = lane_tiles * row_tiles
    share = field.shape[2]
    groups = firsts.shape[0] // pack
    points = orbs.shape[3]

    out[...] = base[0][...] if base else jnp.zeros(out.shape, out.dtype)

    def group_step(group, _):
        parts = []
        for lane_tile in range(lane_tiles):
            rows = []
            for plane in range(planes):
                for row_tile in range(row_tiles):
                    tile = group * per_group + lane_tile * row_tiles + row_tile
                    rows.append(field[tile // share, plane, tile % share])
            parts.append(split_two(jnp.concatenate(rows, axis=0)))
        for couple, start in enumerate(starts):
            high = jnp.concatenate([parts[start][0], parts[start + 1][0]], axis=1)
            low = jnp.concatenate([parts[start][1], parts[start + 1][1]], axis=1)
            half_high, half_low = split_two(
                mxu(high, place_high[couple])
                + mxu(low, place_high[couple])
                + mxu(high, place_low[couple])
            )
            for plane in range(planes):
                span = slice(plane * count, (plane + 1) * count)
                stacked = jnp.concatenate(
                    [half_high[span], half_low[span], half_high[span]], axis=0
                )
                solved = mxu(left[...], stacked)
                for member in range(2):
                    slot = group * pack + 2 * couple + member
                    one, two = firsts[slot], seconds[slot]
                    potential = solved[:, member * points : (member + 1) * points]
                    scale = weights[two]
                    if not base:
                        real = slot < true_pairs
                        scale = jnp.where(real, scale, 0.0)
                        twin = jnp.where(real & (one != two), weights[one], 0.0)
                    out[one, plane] += potential * others[two, plane] * scale
                    if not base:
                        out[two, plane] += potential * orbs[one, plane] * twin
        return 0

    lax.fori_loop(0, groups, group_step, 0)


def spread_form(orbitals, slot_ids, occupations, mode_lists):
    bands, slabs = lax.axis_size("band"), lax.axis_size("slab")
    half = bands // 2
    devices = half * slabs
    points = orbitals.shape[2]
    local = orbitals.shape[0]
    own = local * half
    planes = orbitals.shape[1] // half
    count = mode_lists.shape[1]
    sine_first = sine_table(mode_lists[0], points)
    sine_second = sine_table(mode_lists[1], points)
    sine_third = sine_table(mode_lists[2], points)
    starts, pack, lane_tiles = windows(count)
    row_tiles = count // ROWS
    per_group = lane_tiles * row_tiles
    band, slab = lax.axis_index("band"), lax.axis_index("slab")
    sides = [[side * half + member for member in range(half)] for side in range(2)]
    all_sides = [
        [member * slabs + other for member in side for other in range(slabs)] for side in sides
    ]
    both = ("band", "slab")

    def to_planes(value):
        return lax.all_to_all(
            value, "band", split_axis=1, concat_axis=0, tiled=True, axis_index_groups=sides
        )

    def exchanged(value):
        return lax.all_to_all(
            value, both, split_axis=0, concat_axis=0, tiled=True, axis_index_groups=all_sides
        )

    catalog = jnp.arange(occupations.shape[0], dtype=jnp.int32)
    own_weight = jnp.sum(
        jnp.where(slot_ids[:, None] == catalog[None, :], occupations[None, :], 0.0), axis=1
    )
    weights = lax.all_gather(own_weight, "band", tiled=True).reshape(2, own)
    upper = band >= half
    my_weights = jnp.where(upper, weights[1], weights[0])
    other_weights = jnp.where(upper, weights[0], weights[1]).reshape(half, local)

    orbitals, my_weights, other_weights = lax.optimization_barrier(
        (orbitals, my_weights, other_weights)
    )
    def beside(part, value, work):
        part, value = lax.optimization_barrier((part, value))
        return lax.optimization_barrier((passed_along(part, "band", half), work(value)))

    def parts_of(index):
        cuts = [step * orbitals.shape[1] // 3 for step in range(4)]
        return [
            orbitals[index : index + 1, low:high] for low, high in zip(cuts[:-1], cuts[1:])
        ]

    parts = parts_of(0)
    moved, mine = beside(parts[0], orbitals, to_planes)
    arriving = [moved]

    second_high, second_low = split_table(sine_second)
    empty = jnp.zeros_like(second_low)
    forward_left = jnp.concatenate(
        [
            jnp.concatenate([second_high, second_high], axis=0),
            jnp.concatenate([second_low, empty], axis=0),
        ],
        axis=1,
    ).T
    inverse_left = jnp.concatenate([second_high, second_high, second_low], axis=1)
    placed = []
    block = jnp.kron(jnp.eye(2, dtype=jnp.float32), sine_third.T)
    for couple, start in enumerate(starts):
        above = 2 * couple * count - start * LANES
        placed.append(jnp.pad(block, ((above, 2 * LANES - above - 2 * count), (0, 0))))
    inverse_place = split_table(jnp.stack(placed))
    forward_place = [part.swapaxes(1, 2) for part in inverse_place]

    first_sent = (
        sine_first.reshape(slabs, half, planes, count).swapaxes(0, 1).reshape(points, count)
    )
    squares = [(mode_lists[d] + 1) ** 2 for d in range(3)]
    inner_tiles = (
        squares[1].reshape(1, row_tiles, ROWS, 1)
        + jnp.tile(squares[2], pack).reshape(lane_tiles, 1, 1, LANES)
    ).reshape(per_group, ROWS, LANES)
    device = lax.rem(band, half) * slabs + slab

    vmem = pl.BlockSpec(memory_space=pltpu.VMEM)
    smem = pl.BlockSpec(memory_space=pltpu.SMEM)
    params = pltpu.CompilerParams(vmem_limit_bytes=50 * 2**20)

    def modal(swapped):
        shape = (devices, planes) + swapped.shape[2:]
        share = shape[2]
        rounds = -(-share // per_group) + 1
        inner = lax.dynamic_slice_in_dim(
            jnp.tile(inner_tiles, (rounds, 1, 1)), lax.rem(device * share, per_group), share
        )
        both_squares = (squares[0][:, None] + inner.reshape(1, -1)).astype(jnp.float32)
        screen = 1.0 / (1.0 + both_squares / jnp.float32(points * points))
        flat = swapped.reshape(points, share * ROWS * LANES)
        spectral = screen * jnp.einsum(
            "xm,xa->am", flat, first_sent, precision=lax.Precision.HIGH
        )
        spatial = jnp.einsum("am,xa->xm", spectral, first_sent, precision=lax.Precision.HIGH)
        return exchanged(spatial.reshape(shape))

    def pair_cost(pairs):
        work = pairs * planes * points * points * 2 * LANES * 4
        return pl.CostEstimate(flops=work, bytes_accessed=2**24, transcendentals=0)

    def tables_of(pairs):
        return [jnp.asarray(np.array(part, np.int32)) for part in zip(*pairs)]

    def swapped_of(tables, others):
        groups = tables[0].shape[0] // pack
        share = -(-groups * per_group // devices)
        coeffs = pl.pallas_call(
            forward_kernel,
            out_shape=jax.ShapeDtypeStruct((devices, planes, share, ROWS, LANES), jnp.float32),
            in_specs=[smem] * 2 + [vmem] * 5,
            out_specs=vmem,
            compiler_params=params,
            cost_estimate=pair_cost(tables[0].shape[0]),
        )(*tables, mine, others, forward_left, *forward_place)
        return exchanged(coeffs)

    def terms_of(true_pairs, tables, weights, field, others, base):
        extra = [] if base is None else [base]
        return pl.pallas_call(
            functools.partial(inverse_kernel, true_pairs),
            out_shape=jax.ShapeDtypeStruct(mine.shape, jnp.float32),
            in_specs=[smem] * 3 + [vmem] * (6 + len(extra)),
            out_specs=vmem,
            compiler_params=params,
            cost_estimate=pair_cost(tables[0].shape[0]),
        )(*tables, weights, field, mine, others, *extra, inverse_left, *inverse_place)

    pairs = [(i, j) for i in range(own) for j in range(i, own)]
    true_pairs = len(pairs)
    pairs += [(0, 0)] * (-true_pairs % pack)
    tables = tables_of(pairs)
    moved, swapped = beside(parts[1], mine, lambda value: swapped_of(tables, value))
    arriving.append(moved)
    moved, field = beside(parts[2], swapped, modal)
    arriving.append(moved)
    ready = [(true_pairs, tables, my_weights, field, mine)]
    cross = [(i, j) for i in range(own) for j in range(half)]
    tables = tables_of(cross)
    for k in range(local):
        value = jnp.concatenate(arriving, axis=1)
        parts = parts_of(k + 1) if k + 1 < local else [None] * 3
        arriving = []
        others = None
        for part, work in zip(parts, (to_planes, lambda v: swapped_of(tables, v), modal)):
            if part is None:
                value = work(value)
            else:
                moved, value = beside(part, value, work)
                arriving.append(moved)
            others = value if others is None else others
        ready.append((len(cross), tables, other_weights[:, k], value, others))
    terms = None
    for item in ready:
        terms = terms_of(*item, terms)
    return lax.all_to_all(
        terms, "band", split_axis=0, concat_axis=1, tiled=True, axis_index_groups=sides
    )


def on_device(orbitals, slot_ids, occupations, mode_lists):
    bands = lax.axis_size("band")
    points, count = orbitals.shape[2], mode_lists.shape[1]
    pack = LANES // math.gcd(count, LANES)
    half = bands // 2
    fits = (
        bands % 2 == 0
        and orbitals.shape[1] % half == 0
        and points == LANES
        and count % 16 == 0
        and pack * count >= 2 * LANES
        and (orbitals.shape[0] * half * half) % pack == 0
    )
    form = spread_form if fits else visiting_form
    return form(orbitals, slot_ids, occupations, mode_lists)


def solution(mesh):
    in_specs = (P("band", "slab", None, None), P("band"), P(), P())
    out_specs = P("band", "slab", None, None)
    return jax.shard_map(
        on_device, mesh=mesh, in_specs=in_specs, out_specs=out_specs, check_vma=False
    )
```
